256 devices in a mesh: seq: 16 (over z, core), head: 16 (over y, x).
Axes of the slice: x: 4, y: 4, z: 8, core: 2. Of those that a mesh axis runs over, the one named last changes fastest.
Arguments:
- queries: bfloat16 [49152, 4096], P(('seq', 'head')), may hold values from -6 to 6
- keys: bfloat16 [49152, 4096], P(('seq', 'head')), may hold values from -6 to 6
- values: bfloat16 [49152, 4096], P(('seq', 'head')), may hold values from -6 to 6
- grad_out: bfloat16 [49152, 4096], P(('seq', 'head')), may hold values from -6 to 6
Outputs:
- attended: bfloat16 [49152, 4096], P(('seq', 'head'))
- grad_queries: bfloat16 [49152, 4096], P(('seq', 'head'))
- grad_keys: bfloat16 [49152, 4096], P(('seq', 'head'))
- grad_values: bfloat16 [49152, 4096], P(('seq', 'head'))
The draws below stay inside these ranges and needn't reach their ends.
All inputs are finite; a program needn't handle non-finite values.
Results may differ from the reference program's by a relative error of at most 0.005.
Values may be sent and summed in bfloat16 or wider, within the bound.
A program may use at most 128 MiB of HBM per device.

```python
import math
import jax
import jax.numpy as jnp
from jax import lax

HEADS = 32
HD = 128
BLOCK = 256
SEQ = 49152


def level_of(key, extent, pieces, low, high):
    loudness = 1.0
    for dim, parts in pieces:
        draws = jax.random.uniform(jax.random.fold_in(jax.random.fold_in(key, 6), dim), (parts,), jnp.float32, low / len(pieces), high / len(pieces))
        loudness = loudness * jnp.repeat(jnp.exp(draws), extent[dim] // parts).reshape((-1,) + (1,) * (len(extent) - 1 - dim))
    return loudness


def bell_draw(stream_key, shape, width, most, split=(), dtype=jnp.bfloat16):
    result = width * jax.random.normal(stream_key, shape, jnp.float32)
    if split:
        result = result * level_of(stream_key, shape, split, -0.22, 0.18)
    return jnp.clip(result, -most, most).astype(dtype)


def setup_inputs(seed: int = 0) -> dict:
    splits = jax.random.split(jax.random.key(seed), 5)
    return {
        "queries": bell_draw(splits[0], (SEQ, HEADS * HD), 1.0, 6.0, ((0, 256),)),
        "keys": bell_draw(splits[1], (SEQ, HEADS * HD), 1.0, 6.0, ((0, 256),)),
        "values": bell_draw(splits[2], (SEQ, HEADS * HD), 1.0, 6.0, ((0, 256),)),
        "grad_out": bell_draw(splits[3], (SEQ, HEADS * HD), 1.0, 6.0, ((0, 256),)),
    }


def to_float(x):
    return x.astype(jnp.float32)

def rounded(x):
    return to_float(lax.optimization_barrier(x.astype(jnp.bfloat16)))

def block_scores(qf, kf, gf, vf):
    mask = jnp.tril(jnp.ones((BLOCK, BLOCK), jnp.float32))
    hi = lax.Precision.HIGHEST
    qk = rounded(jnp.einsum('thd,shd->hts', qf, kf, precision=hi) * mask)
    gv = rounded(jnp.einsum('thd,shd->hts', gf, vf, precision=hi) * mask)
    return (qk, gv)

def reference(queries, keys, values, grad_out):
    hi = lax.Precision.HIGHEST
    scale = 1.0 / math.sqrt(HD * SEQ)
    blocks = SEQ // BLOCK
    shape4 = (blocks, BLOCK, HEADS, HD)
    qs = queries.reshape(shape4)
    ks = keys.reshape(shape4)
    vs = values.reshape(shape4)
    gs = grad_out.reshape(shape4)

    def forward_step(state, block):
        qb, kb, vb, gb = block
        qf, kf, vf, gf = (to_float(qb), to_float(kb), to_float(vb), to_float(gb))
        qk, gv = block_scores(qf, kf, gf, vf)
        sb = rounded(state)
        out = scale * (jnp.einsum('hts,shd->thd', qk, vf, precision=hi) + jnp.einsum('thd,hde->the', qf, sb, precision=hi))
        dq = scale * (jnp.einsum('hts,shd->thd', gv, kf, precision=hi) + jnp.einsum('thi,hji->thj', gf, sb, precision=hi))
        state = state + jnp.einsum('shd,she->hde', kf, vf, precision=hi)
        return (state, (out.astype(jnp.bfloat16), dq.astype(jnp.bfloat16)))

    def backward_step(state, block):
        qb, kb, vb, gb = block
        qf, kf, vf, gf = (to_float(qb), to_float(kb), to_float(vb), to_float(gb))
        qk, gv = block_scores(qf, kf, gf, vf)
        rb = rounded(state)
        dk = scale * (jnp.einsum('hts,thd->shd', gv, qf, precision=hi) + jnp.einsum('shi,hij->shj', vf, rb, precision=hi))
        dv = scale * (jnp.einsum('hts,thi->shi', qk, gf, precision=hi) + jnp.einsum('shj,hij->shi', kf, rb, precision=hi))
        state = state + jnp.einsum('thi,thj->hij', gf, qf, precision=hi)
        return (state, (dk.astype(jnp.bfloat16), dv.astype(jnp.bfloat16)))
    start = jnp.zeros((HEADS, HD, HD), jnp.float32)
    final_a, (outs, dqs) = lax.scan(forward_step, start, (qs, ks, vs, gs))
    final_b, (dks, dvs) = lax.scan(backward_step, start, (qs, ks, vs, gs), reverse=True)
    flat = (SEQ, HEADS * HD)
    return (outs.reshape(flat), dqs.reshape(flat), dks.reshape(flat), dvs.reshape(flat))
```

```python
import functools
import math

import jax
import jax.numpy as jnp
from jax import lax
from jax.experimental import pallas as pl
from jax.experimental.pallas import tpu as pltpu
from jax.sharding import PartitionSpec as P

HD = 128
NH = 16
NZ = 8
NC = 2
CH = 4
F32 = jnp.float32
BF16 = jnp.bfloat16
MESH = pl.DeviceIdType.MESH


PLAN = (
    ("L", 0), ("A", 0), ("C", 0), ("L", 1), ("A", 1), ("D", 0), ("C", 1), ("E", 0),
    ("A", 2), ("D", 1), ("C", 2), ("E", 1), ("L", 2), ("A", 3), ("D", 2), ("C", 3), ("E", 2),
    ("D", 3), ("E", 3), ("L", 3), ("G", 0), ("G", 1), ("G", 2), ("G", 3),
)


def contract(a, b, da, db):
    return lax.dot_general(a, b, (((da,), (db,)), ((), ())), preferred_element_type=F32)


def kernel(
    scale,
    q_hbm, k_hbm, v_hbm, g_hbm,
    a_hbm, dq_hbm, dk_hbm, dv_hbm,
    x4, loc, out4,
    mine, xr, xb, xp,
    cs, cr, zs, zr, ds, dr,
    in_sem, out_sem,
    x1s, x1r, c1s, c1r, zss, zrs, c2s, c2r, x2s, x2r,
):
    seq = lax.axis_index("seq")
    head = lax.axis_index("head")
    z = seq // NC
    core = lax.rem(seq, NC)
    chunks = xr.shape[0]
    rows = xr.shape[3]
    tokens = x4.shape[1]
    wide = x4.shape[2] // chunks
    pair = 2 * HD

    ins = (q_hbm, k_hbm, v_hbm, g_hbm)
    outs = (a_hbm, dq_hbm, dk_hbm, dv_hbm)

    def load(c, i):
        cols = pl.ds(c * wide, wide)
        return pltpu.make_async_copy(ins[i].at[:, cols], x4.at[i, :, cols], in_sem.at[c, i])

    def store(c, i):
        cols = pl.ds(c * wide, wide)
        return pltpu.make_async_copy(out4.at[i, :, cols], outs[i].at[:, cols], out_sem.at[c, i])

    def at_z(to):
        return (to * NC + core, head)

    other = (z * NC + 1 - core, head)

    def remote(src, dst, send, recv, to):
        return pltpu.make_async_remote_copy(src, dst, send, recv, device_id=to, device_id_type=MESH)

    def ahead(d):
        return lax.rem(head + d, NH)

    def slot(i):
        return lax.rem(head + NH - i, NH)

    def x_out(c, d):
        to = ahead(d)
        return remote(mine.at[c, to], xr.at[c, d], x1s.at[c], x1r.at[c], (seq, to))

    def xb_out(c, d):
        to = ahead(d)
        return remote(xb.at[c, to], xp.at[c, head], x2s.at[c], x2r.at[c], (seq, to))

    def x_all(c):
        some = pl.ds(1, NH - 1)
        return remote(mine.at[c, some], xr.at[c, some], x1s.at[c], x1r.at[c], (seq, ahead(1)))

    def xb_all(c):
        some = pl.ds(1, NH - 1)
        return remote(xb.at[c, some], xp.at[c, some], x2s.at[c], x2r.at[c], (seq, ahead(1)))

    def c_swap(c):
        return remote(cs.at[c, 1 - core], cr.at[c], c1s.at[c], c1r.at[c], other)

    def z_out(c, to):
        return remote(zs.at[c], zr.at[c, z], zss.at[c, to], zrs.at[c, z], at_z(to))

    def z_in(c, frm):
        return remote(zs.at[c], zr.at[c, frm], zss.at[c, frm], zrs.at[c, frm], at_z(frm))

    def d_swap(c):
        return remote(ds.at[c], dr.at[c], c2s.at[c], c2r.at[c], other)

    def sends_to(to):
        return jnp.logical_or(
            jnp.logical_and(core == 0, to > z), jnp.logical_and(core == 1, to < z)
        )

    def hears_from(frm):
        return jnp.logical_or(
            jnp.logical_and(core == 0, frm < z), jnp.logical_and(core == 1, frm > z)
        )

    barrier = pltpu.get_barrier_semaphore()

    def greet(to):
        pl.semaphore_signal(barrier, inc=1, device_id=to, device_id_type=MESH)

    for d in range(1, NH):
        greet((seq, ahead(d)))
    for d in range(1, NZ):
        greet(at_z(lax.rem(z + d, NZ)))
    greet(other)

    for c in range(chunks):
        for i in range(4):
            load(c, i).start()

    def part(ref, j):
        return ref[:, j * HD : (j + 1) * HD]

    def each_pair(c, act):
        def body(o, carry):
            cols = pl.ds(pl.multiple_of(c * wide + o * pair, pair), pair)
            act(o, cols, [x4[i, :, cols] for i in range(4)])
            return carry

        lax.fori_loop(0, wide // pair, body, 0)

    slots = HD // rows

    def local_states(c):
        def act(o, cols, qkvg):
            q, k, v, g = qkvg
            for j in range(2):
                kv = contract(part(k, j), part(v, j), 0, 0).astype(BF16)
                rq = contract(part(g, j), part(q, j), 0, 0).astype(BF16)
                for r in range(slots):
                    at = (o * 2 + j) * slots + r
                    mine[c, at, 0] = kv[r * rows : (r + 1) * rows]
                    mine[c, at, 1] = rq[r * rows : (r + 1) * rows]

        each_pair(c, act)

    def local_attention(c):
        t = lax.broadcasted_iota(jnp.int32, (tokens, tokens), 0)
        s = lax.broadcasted_iota(jnp.int32, (tokens, tokens), 1)

        def act(o, cols, qkvg):
            zero = jnp.zeros((tokens, tokens), F32)
            for j in range(2):
                qj, kj, vj, gj = (part(r, j) for r in qkvg)
                here = pl.ds(pl.multiple_of(c * wide + o * pair + j * HD, HD), HD)
                qk = jnp.where(t >= s, contract(qj, kj, 1, 1), zero).astype(BF16)
                loc[0, :, here] = contract(qk, vj, 1, 0)
                gv = jnp.where(t >= s, contract(gj, vj, 1, 1), zero).astype(BF16)
                loc[1, :, here] = contract(gv, kj, 1, 0)
                vg = jnp.where(s >= t, contract(vj, gj, 1, 1), zero).astype(BF16)
                loc[2, :, here] = contract(vg, qj, 1, 0)
                kq = jnp.where(s >= t, contract(kj, qj, 1, 1), zero).astype(BF16)
                loc[3, :, here] = contract(kq, gj, 1, 0)

        each_pair(c, act)

    def finish(c):
        def act(o, cols, qkvg):
            q, k, v, g = qkvg
            for j in range(2):
                here = pl.ds(pl.multiple_of(c * wide + o * pair + j * HD, HD), HD)
                at = pl.ds((o * 2 + j) * slots, slots)
                kv = xp[c, at, 0].reshape(HD, HD)
                rq = xp[c, at, 1].reshape(HD, HD)
                terms = (
                    contract(part(q, j), kv, 1, 0),
                    contract(part(g, j), kv, 1, 1),
                    contract(part(v, j), rq, 1, 0),
                    contract(part(k, j), rq, 1, 1),
                )
                for i in range(4):
                    out4[i, :, here] = (scale * (loc[i, :, here] + terms[i])).astype(BF16)

        each_pair(c, act)

    def stage_a(c):
        xr[c, 0] = mine[c, head]
        x_all(c).wait_recv()
        total = xr[c, 0].astype(F32)
        for d in range(1, NH):
            total += xr[c, d].astype(F32)
        cs[c] = total
        c_swap(c).start()

    def stage_c(c):
        c_swap(c).wait_recv()
        zs[c] = cs[c, core] + cr[c]
        for i in range(NZ):
            @pl.when(sends_to(i))
            def _():
                z_out(c, i).start()

    def stage_d(c):
        ds[c] = jnp.zeros_like(ds[c])
        for i in range(NZ):
            @pl.when(hears_from(i))
            def _():
                z_in(c, i).wait_recv()
                ds[c] += zr[c, i]
        zr[c, z] = ds[c]
        ds[c] += cs[c, core]
        d_swap(c).start()

    def stage_e(c):
        d_swap(c).wait_recv()
        for kind in range(2):
            base = jnp.where(core == kind, zr[c, z], dr[c])
            order = range(NH) if kind == 0 else range(NH - 1, -1, -1)
            for i in order:
                xb[c, i, kind] = base.astype(BF16)
                base = base + xr[c, slot(i), kind].astype(F32)
        for d in range(1, NH):
            xb_out(c, d).start()
        xp[c, head] = xb[c, head]

    def stage_g(c):
        xb_all(c).wait_recv()
        finish(c)
        for i in range(4):
            store(c, i).start()

    for c in range(chunks):
        for i in range(4):
            load(c, i).wait()
        local_states(c)
        if c == 0:
            pl.semaphore_wait(barrier, NH + NZ - 1)
        for d in range(1, NH):
            x_out(c, d).start()

    stages = {
        "L": local_attention, "A": stage_a, "C": stage_c, "D": stage_d, "E": stage_e, "G": stage_g,
    }
    for name, c in PLAN:
        stages[name](c)

    for c in range(chunks):
        x_all(c).wait_send()
        c_swap(c).wait_send()
        for i in range(NZ):
            @pl.when(sends_to(i))
            def _():
                z_out(c, i).wait_send()
        d_swap(c).wait_send()
        xb_all(c).wait_send()
        for i in range(4):
            store(c, i).wait()


def on_device(queries, keys, values, grad_out):
    tokens, width = queries.shape
    heads = width // HD
    rows = heads // CH * HD // NH
    devices = lax.axis_size("seq") * lax.axis_size("head")
    scale = 1.0 / math.sqrt(HD * tokens * devices)
    shift = 2.0 ** math.floor(math.log2(scale))
    state = (CH, NH, 2, rows, HD)
    piece = (rows, HD)
    vmem = pltpu.VMEM
    dma = pltpu.SemaphoreType.DMA
    anywhere = pl.BlockSpec(memory_space=pl.ANY)
    macs = tokens * heads * (8 * tokens * HD + 6 * HD * HD)
    results = pl.pallas_call(
        functools.partial(kernel, scale / shift),
        out_shape=[jax.ShapeDtypeStruct((tokens, width), BF16)] * 4,
        in_specs=[anywhere] * 4,
        out_specs=[anywhere] * 4,
        scratch_shapes=[
            vmem((4, tokens, width), BF16),
            vmem((4, tokens, width), F32),
            vmem((4, tokens, width), BF16),
            vmem(state, BF16), vmem(state, BF16), vmem(state, BF16), vmem(state, BF16),
            vmem((CH, 2) + piece, F32), vmem((CH,) + piece, F32),
            vmem((CH,) + piece, F32), vmem((CH, NZ) + piece, F32),
            vmem((CH,) + piece, F32), vmem((CH,) + piece, F32),
            dma((CH, 4)), dma((CH, 4)),
            dma((CH,)), dma((CH,)),
            dma((CH,)), dma((CH,)),
            dma((CH, NZ)), dma((CH, NZ)),
            dma((CH,)), dma((CH,)),
            dma((CH,)), dma((CH,)),
        ],
        compiler_params=pltpu.CompilerParams(
            collective_id=0, has_side_effects=True, vmem_limit_bytes=58 * 2**20
        ),
        cost_estimate=pl.CostEstimate(
            flops=2 * macs, bytes_accessed=16 * tokens * width, transcendentals=0
        ),
    )(queries, keys, values, grad_out)
    return tuple(r * jnp.asarray(shift, BF16) for r in results)


def solution(mesh):
    spec = P(("seq", "head"), None)
    return jax.shard_map(
        on_device, mesh=mesh, in_specs=(spec,) * 4, out_specs=(spec,) * 4, check_vma=False
    )
```

```python
import functools
import math

import jax
import jax.numpy as jnp
from jax import lax
from jax.experimental import pallas as pl
from jax.experimental.pallas import tpu as pltpu
from jax.sharding import PartitionSpec as P

HD = 128
NH = 16
NZ = 8
NC = 2
CH = 4
F32 = jnp.float32
BF16 = jnp.bfloat16
MESH = pl.DeviceIdType.MESH


PLAN = (
    ("L", 0), ("A", 0), ("C", 0), ("L", 1), ("A", 1), ("D", 0), ("C", 1), ("E", 0),
    ("A", 2), ("D", 1), ("C", 2), ("E", 1), ("L", 2), ("A", 3), ("D", 2), ("C", 3), ("E", 2),
    ("D", 3), ("E", 3), ("L", 3), ("G", 0), ("G", 1), ("G", 2), ("G", 3),
)


def contract(a, b, da, db):
    return lax.dot_general(a, b, (((da,), (db,)), ((), ())), preferred_element_type=F32)


def kernel(
    scale,
    q_hbm, k_hbm, v_hbm, g_hbm,
    a_out, dq_out, dk_out, dv_out,
    x4, loc,
    mine, xr, xb, xp,
    cs, cr, zs, zr, ds, dr,
    in_sem,
    x1s, x1r, c1s, c1r, zss, zrs, c2s, c2r, x2s, x2r,
):
    seq = lax.axis_index("seq")
    head = lax.axis_index("head")
    z = seq // NC
    core = lax.rem(seq, NC)
    chunks = xr.shape[0]
    rows = xr.shape[3]
    tokens = x4.shape[1]
    wide = x4.shape[2] // chunks
    pair = 2 * HD

    ins = (q_hbm, k_hbm, v_hbm, g_hbm)
    outs = (a_out, dq_out, dk_out, dv_out)

    def load(c, i):
        cols = pl.ds(c * wide, wide)
        return pltpu.make_async_copy(ins[i].at[:, cols], x4.at[i, :, cols], in_sem.at[c, i])

    def at_z(to):
        return (to * NC + core, head)

    other = (z * NC + 1 - core, head)

    def remote(src, dst, send, recv, to):
        return pltpu.make_async_remote_copy(src, dst, send, recv, device_id=to, device_id_type=MESH)

    def ahead(d):
        return lax.rem(head + d, NH)

    def slot(i):
        return lax.rem(head + NH - i, NH)

    def x_out(c, d):
        to = ahead(d)
        return remote(mine.at[c, to], xr.at[c, d], x1s.at[c], x1r.at[c], (seq, to))

    def xb_out(c, d):
        to = ahead(d)
        return remote(xb.at[c, to], xp.at[c, head], x2s.at[c], x2r.at[c], (seq, to))

    def x_all(c):
        some = pl.ds(1, NH - 1)
        return remote(mine.at[c, some], xr.at[c, some], x1s.at[c], x1r.at[c], (seq, ahead(1)))

    def xb_all(c):
        some = pl.ds(1, NH - 1)
        return remote(xb.at[c, some], xp.at[c, some], x2s.at[c], x2r.at[c], (seq, ahead(1)))

    def c_swap(c):
        return remote(cs.at[c, 1 - core], cr.at[c], c1s.at[c], c1r.at[c], other)

    def z_out(c, to):
        return remote(zs.at[c], zr.at[c, z], zss.at[c, to], zrs.at[c, z], at_z(to))

    def z_in(c, frm):
        return remote(zs.at[c], zr.at[c, frm], zss.at[c, frm], zrs.at[c, frm], at_z(frm))

    def d_swap(c):
        return remote(ds.at[c], dr.at[c], c2s.at[c], c2r.at[c], other)

    def sends_to(to):
        return jnp.logical_or(
            jnp.logical_and(core == 0, to > z), jnp.logical_and(core == 1, to < z)
        )

    def hears_from(frm):
        return jnp.logical_or(
            jnp.logical_and(core == 0, frm < z), jnp.logical_and(core == 1, frm > z)
        )

    barrier = pltpu.get_barrier_semaphore()

    def greet(to):
        pl.semaphore_signal(barrier, inc=1, device_id=to, device_id_type=MESH)

    for d in range(1, NH):
        greet((seq, ahead(d)))
    for d in range(1, NZ):
        greet(at_z(lax.rem(z + d, NZ)))
    greet(other)

    for c in range(chunks):
        for i in range(4):
            load(c, i).start()

    def part(ref, j):
        return ref[:, j * HD : (j + 1) * HD]

    def each_pair(c, act):
        def body(o, carry):
            cols = pl.ds(pl.multiple_of(c * wide + o * pair, pair), pair)
            act(o, cols, [x4[i, :, cols] for i in range(4)])
            return carry

        lax.fori_loop(0, wide // pair, body, 0)

    slots = HD // rows

    def local_states(c):
        def act(o, cols, qkvg):
            q, k, v, g = qkvg
            for j in range(2):
                kv = contract(part(k, j), part(v, j), 0, 0).astype(BF16)
                rq = contract(part(g, j), part(q, j), 0, 0).astype(BF16)
                for r in range(slots):
                    at = (o * 2 + j) * slots + r
                    mine[c, at, 0] = kv[r * rows : (r + 1) * rows]
                    mine[c, at, 1] = rq[r * rows : (r + 1) * rows]

        each_pair(c, act)

    def local_attention(c):
        t = lax.broadcasted_iota(jnp.int32, (tokens, tokens), 0)
        s = lax.broadcasted_iota(jnp.int32, (tokens, tokens), 1)

        def act(o, cols, qkvg):
            zero = jnp.zeros((tokens, tokens), F32)
            for j in range(2):
                qj, kj, vj, gj = (part(r, j) for r in qkvg)
                here = pl.ds(pl.multiple_of(c * wide + o * pair + j * HD, HD), HD)
                qk = jnp.where(t >= s, contract(qj, kj, 1, 1), zero).astype(BF16)
                loc[0, :, here] = contract(qk, vj, 1, 0)
                gv = jnp.where(t >= s, contract(gj, vj, 1, 1), zero).astype(BF16)
                loc[1, :, here] = contract(gv, kj, 1, 0)
                vg = jnp.where(s >= t, contract(vj, gj, 1, 1), zero).astype(BF16)
                loc[2, :, here] = contract(vg, qj, 1, 0)
                kq = jnp.where(s >= t, contract(kj, qj, 1, 1), zero).astype(BF16)
                loc[3, :, here] = contract(kq, gj, 1, 0)

        each_pair(c, act)

    def finish(c):
        def act(o, cols, qkvg):
            q, k, v, g = qkvg
            for j in range(2):
                here = pl.ds(pl.multiple_of(c * wide + o * pair + j * HD, HD), HD)
                at = pl.ds((o * 2 + j) * slots, slots)
                kv = xp[c, at, 0].reshape(HD, HD)
                rq = xp[c, at, 1].reshape(HD, HD)
                terms = (
                    contract(part(q, j), kv, 1, 0),
                    contract(part(g, j), kv, 1, 1),
                    contract(part(v, j), rq, 1, 0),
                    contract(part(k, j), rq, 1, 1),
                )
                for i in range(4):
                    outs[i][:, here] = (scale * (loc[i, :, here] + terms[i])).astype(BF16)

        each_pair(c, act)

    def stage_a(c):
        xr[c, 0] = mine[c, head]
        x_all(c).wait_recv()
        total = xr[c, 0].astype(F32)
        for d in range(1, NH):
            total += xr[c, d].astype(F32)
        cs[c] = total
        c_swap(c).start()

    def stage_c(c):
        c_swap(c).wait_recv()
        zs[c] = cs[c, core] + cr[c]
        for i in range(NZ):
            @pl.when(sends_to(i))
            def _():
                z_out(c, i).start()

    def stage_d(c):
        ds[c] = jnp.zeros_like(ds[c])
        for i in range(NZ):
            @pl.when(hears_from(i))
            def _():
                z_in(c, i).wait_recv()
                ds[c] += zr[c, i]
        zr[c, z] = ds[c]
        ds[c] += cs[c, core]
        d_swap(c).start()

    def stage_e(c):
        d_swap(c).wait_recv()
        for kind in range(2):
            base = jnp.where(core == kind, zr[c, z], dr[c])
            order = range(NH) if kind == 0 else range(NH - 1, -1, -1)
            for i in order:
                xb[c, i, kind] = base.astype(BF16)
                base = base + xr[c, slot(i), kind].astype(F32)
        for d in range(1, NH):
            xb_out(c, d).start()
        xp[c, head] = xb[c, head]

    def stage_g(c):
        xb_all(c).wait_recv()
        finish(c)

    for c in range(chunks):
        for i in range(4):
            load(c, i).wait()
        local_states(c)
        if c == 0:
            pl.semaphore_wait(barrier, NH + NZ - 1)
        for d in range(1, NH):
            x_out(c, d).start()

    stages = {
        "L": local_attention, "A": stage_a, "C": stage_c, "D": stage_d, "E": stage_e, "G": stage_g,
    }
    for name, c in PLAN:
        stages[name](c)

    for c in range(chunks):
        x_all(c).wait_send()
        c_swap(c).wait_send()
        for i in range(NZ):
            @pl.when(sends_to(i))
            def _():
                z_out(c, i).wait_send()
        d_swap(c).wait_send()
        xb_all(c).wait_send()


def on_device(queries, keys, values, grad_out):
    tokens, width = queries.shape
    heads = width // HD
    rows = heads // CH * HD // NH
    devices = lax.axis_size("seq") * lax.axis_size("head")
    scale = 1.0 / math.sqrt(HD * tokens * devices)
    shift = 2.0 ** math.floor(math.log2(scale))
    state = (CH, NH, 2, rows, HD)
    piece = (rows, HD)
    vmem = pltpu.VMEM
    dma = pltpu.SemaphoreType.DMA
    anywhere = pl.BlockSpec(memory_space=pl.ANY)
    macs = tokens * heads * (8 * tokens * HD + 6 * HD * HD)
    results = pl.pallas_call(
        functools.partial(kernel, scale / shift),
        out_shape=[pltpu.VMEM((tokens, width), BF16)] * 4,
        in_specs=[anywhere] * 4,
        scratch_shapes=[
            vmem((4, tokens, width), BF16),
            vmem((4, tokens, width), F32),
            vmem(state, BF16), vmem(state, BF16), vmem(state, BF16), vmem(state, BF16),
            vmem((CH, 2) + piece, F32), vmem((CH,) + piece, F32),
            vmem((CH,) + piece, F32), vmem((CH, NZ) + piece, F32),
            vmem((CH,) + piece, F32), vmem((CH,) + piece, F32),
            dma((CH, 4)),
            dma((CH,)), dma((CH,)),
            dma((CH,)), dma((CH,)),
            dma((CH, NZ)), dma((CH, NZ)),
            dma((CH,)), dma((CH,)),
            dma((CH,)), dma((CH,)),
        ],
        compiler_params=pltpu.CompilerParams(
            collective_id=0, has_side_effects=True, vmem_limit_bytes=54 * 2**20
        ),
        cost_estimate=pl.CostEstimate(
            flops=2 * macs, bytes_accessed=16 * tokens * width, transcendentals=0
        ),
    )(queries, keys, values, grad_out)
    return tuple(r * jnp.asarray(shift, BF16) for r in results)


def solution(mesh):
    spec = P(("seq", "head"), None)
    return jax.shard_map(
        on_device, mesh=mesh, in_specs=(spec,) * 4, out_specs=(spec,) * 4, check_vma=False
    )
```

```python
import functools
import math

import jax
import jax.numpy as jnp
from jax import lax
from jax.experimental import pallas as pl
from jax.experimental.pallas import tpu as pltpu
from jax.sharding import PartitionSpec as P

HD = 128
NX = 4
NY = 4
NH = NX * NY
NZ = 8
NC = 2
CH = 4
F32 = jnp.float32
BF16 = jnp.bfloat16
MESH = pl.DeviceIdType.MESH


ORDER = (10, 6, 9, 14, 11, 5, 15, 7, 13, 2, 8, 1, 3, 4, 12)
PLAN = (
    ("L", 0), ("A", 0), ("C", 0), ("L", 1), ("A", 1), ("C", 1), ("D", 0), ("E", 0),
    ("A", 2), ("C", 2), ("D", 1), ("E", 1), ("L", 2), ("A", 3), ("C", 3), ("D", 2),
    ("E", 2), ("D", 3), ("E", 3), ("L", 3), ("G", 0), ("G", 1), ("G", 2), ("G", 3),
)


def contract(a, b, da, db):
    return lax.dot_general(a, b, (((da,), (db,)), ((), ())), preferred_element_type=F32)


def kernel(
    scale,
    q_hbm, k_hbm, v_hbm, g_hbm,
    a_out, dq_out, dk_out, dv_out,
    x4, loc,
    mine, xr, xb, xp,
    cs, cr, zs, zr, ds, dr,
    in_sem, told,
    x1s, x1r, c1s, c1r, zss, zrs, c2s, c2r, x2s, x2r,
):
    seq = lax.axis_index("seq")
    head = lax.axis_index("head")
    z = seq // NC
    core = lax.rem(seq, NC)
    y = head // NX
    x = lax.rem(head, NX)
    chunks = xr.shape[0]
    rows = xr.shape[3]
    tokens = x4.shape[1]
    wide = x4.shape[2] // chunks
    pair = 2 * HD

    ins = (q_hbm, k_hbm, v_hbm, g_hbm)
    outs = (a_out, dq_out, dk_out, dv_out)

    def load(c, i):
        cols = pl.ds(c * wide, wide)
        return pltpu.make_async_copy(ins[i].at[:, cols], x4.at[i, :, cols], in_sem.at[c, i])

    def at_z(to):
        return (to * NC + core, head)

    other = (z * NC + 1 - core, head)

    def remote(src, dst, send, recv, to):
        return pltpu.make_async_remote_copy(src, dst, send, recv, device_id=to, device_id_type=MESH)

    def ahead(d):
        return lax.rem(y + d // NX, NY) * NX + lax.rem(x + d % NX, NX)

    def slot(i):
        return lax.rem(y + NY - i // NX, NY) * NX + lax.rem(x + NX - i % NX, NX)

    def x_out(c, d):
        to = ahead(d)
        return remote(mine.at[c, to], xr.at[c, d], x1s.at[c], x1r.at[c], (seq, to))

    def xb_out(c, d):
        to = ahead(d)
        return remote(xb.at[c, to], xp.at[c, head], x2s.at[c], x2r.at[c], (seq, to))

    def x_all(c):
        some = pl.ds(1, NH - 1)
        return remote(mine.at[c, some], xr.at[c, some], x1s.at[c], x1r.at[c], (seq, ahead(1)))

    def xb_all(c):
        some = pl.ds(1, NH - 1)
        return remote(xb.at[c, some], xp.at[c, some], x2s.at[c], x2r.at[c], (seq, ahead(1)))

    def c_swap(c):
        return remote(cs.at[c, 1 - core], cr.at[c], c1s.at[c], c1r.at[c], other)

    def z_out(c, to):
        return remote(zs.at[c], zr.at[c, z], zss.at[c, to], zrs.at[c, z], at_z(to))

    def z_in(c, frm):
        return remote(zs.at[c], zr.at[c, frm], zss.at[c, frm], zrs.at[c, frm], at_z(frm))

    def d_swap(c):
        return remote(ds.at[c], dr.at[c], c2s.at[c], c2r.at[c], other)

    def sends_to(to):
        return jnp.logical_or(
            jnp.logical_and(core == 0, to > z), jnp.logical_and(core == 1, to < z)
        )

    def hears_from(frm):
        return jnp.logical_or(
            jnp.logical_and(core == 0, frm < z), jnp.logical_and(core == 1, frm > z)
        )

    barrier = pltpu.get_barrier_semaphore()

    def greet(to):
        pl.semaphore_signal(barrier, inc=1, device_id=to, device_id_type=MESH)

    for d in range(1, NH):
        greet((z * NC, ahead(d)))
    for d in range(1, NZ):
        greet((lax.rem(z + d, NZ) * NC + 1, head))
    greet(other)

    for c in range(chunks):
        for i in range(4):
            load(c, i).start()

    def part(ref, j):
        return ref[:, j * HD : (j + 1) * HD]

    def each_pair(c, act):
        def body(o, carry):
            cols = pl.ds(pl.multiple_of(c * wide + o * pair, pair), pair)
            act(o, cols, [x4[i, :, cols] for i in range(4)])
            return carry

        lax.fori_loop(0, wide // pair, body, 0)

    slots = HD // rows

    def local_states(c):
        def act(o, cols, qkvg):
            q, k, v, g = qkvg
            for j in range(2):
                kv = contract(part(k, j), part(v, j), 0, 0).astype(BF16)
                rq = contract(part(g, j), part(q, j), 0, 0).astype(BF16)
                for r in range(slots):
                    at = (o * 2 + j) * slots + r
                    mine[c, at, 0] = kv[r * rows : (r + 1) * rows]
                    mine[c, at, 1] = rq[r * rows : (r + 1) * rows]

        each_pair(c, act)

    def local_attention(c):
        t = lax.broadcasted_iota(jnp.int32, (tokens, tokens), 0)
        s = lax.broadcasted_iota(jnp.int32, (tokens, tokens), 1)

        def act(o, cols, qkvg):
            zero = jnp.zeros((tokens, tokens), F32)
            for j in range(2):
                qj, kj, vj, gj = (part(r, j) for r in qkvg)
                here = pl.ds(pl.multiple_of(c * wide + o * pair + j * HD, HD), HD)
                qk = jnp.where(t >= s, contract(qj, kj, 1, 1), zero).astype(BF16)
                loc[0, :, here] = contract(qk, vj, 1, 0)
                gv = jnp.where(t >= s, contract(gj, vj, 1, 1), zero).astype(BF16)
                loc[1, :, here] = contract(gv, kj, 1, 0)
                vg = jnp.where(s >= t, contract(vj, gj, 1, 1), zero).astype(BF16)
                loc[2, :, here] = contract(vg, qj, 1, 0)
                kq = jnp.where(s >= t, contract(kj, qj, 1, 1), zero).astype(BF16)
                loc[3, :, here] = contract(kq, gj, 1, 0)

        each_pair(c, act)

    def finish(c):
        def act(o, cols, qkvg):
            q, k, v, g = qkvg
            for j in range(2):
                here = pl.ds(pl.multiple_of(c * wide + o * pair + j * HD, HD), HD)
                at = pl.ds((o * 2 + j) * slots, slots)
                kv = xp[c, at, 0].reshape(HD, HD)
                rq = xp[c, at, 1].reshape(HD, HD)
                terms = (
                    contract(part(q, j), kv, 1, 0),
                    contract(part(g, j), kv, 1, 1),
                    contract(part(v, j), rq, 1, 0),
                    contract(part(k, j), rq, 1, 1),
                )
                for i in range(4):
                    outs[i][:, here] = (scale * (loc[i, :, here] + terms[i])).astype(BF16)

        each_pair(c, act)

    def stage_a(c):
        xr[c, 0] = mine[c, head]
        x_all(c).wait_recv()
        total = xr[c, 0].astype(F32)
        for d in range(1, NH):
            total += xr[c, d].astype(F32)
        cs[c] = total
        c_swap(c).start()

    def stage_c(c):
        c_swap(c).wait_recv()
        zs[c] = cs[c, core] + cr[c]
        for i in range(NZ):
            @pl.when(sends_to(i))
            def _():
                z_out(c, i).start()

    def stage_d(c):
        ds[c] = jnp.zeros_like(ds[c])
        for i in range(NZ):
            @pl.when(hears_from(i))
            def _():
                z_in(c, i).wait_recv()
                ds[c] += zr[c, i]
        zr[c, z] = ds[c]
        ds[c] += cs[c, core]
        d_swap(c).start()

    def stage_e(c):
        d_swap(c).wait_recv()
        for kind in range(2):
            base = jnp.where(core == kind, zr[c, z], dr[c])
            order = range(NH) if kind == 0 else range(NH - 1, -1, -1)
            for i in order:
                xb[c, i, kind] = base.astype(BF16)
                base = base + xr[c, slot(i), kind].astype(F32)
        for d in ORDER:
            xb_out(c, d).start()
        xp[c, head] = xb[c, head]

    def stage_g(c):
        xb_all(c).wait_recv()
        finish(c)

    for c in range(chunks):
        for i in range(4):
            load(c, i).wait()
        local_states(c)
        if c == 0:
            @pl.when(core == 0)
            def _():
                pl.semaphore_wait(barrier, NC * (NH - 1) + 1)
                pl.semaphore_signal(told, inc=1, device_id=other, device_id_type=MESH)

            @pl.when(core == 1)
            def _():
                pl.semaphore_wait(told, 1)

        for d in ORDER:
            x_out(c, d).start()

    stages = {
        "L": local_attention, "A": stage_a, "C": stage_c, "D": stage_d, "E": stage_e, "G": stage_g,
    }
    def meet_z():
        @pl.when(core == 1)
        def _():
            pl.semaphore_wait(barrier, NC * (NZ - 1) + 1)
            pl.semaphore_signal(told, inc=1, device_id=other, device_id_type=MESH)

        @pl.when(core == 0)
        def _():
            pl.semaphore_wait(told, 1)

    for name, c in PLAN:
        if (name, c) == ("A", 0):
            meet_z()
        stages[name](c)

    for c in range(chunks):
        x_all(c).wait_send()
        c_swap(c).wait_send()
        for i in range(NZ):
            @pl.when(sends_to(i))
            def _():
                z_out(c, i).wait_send()
        d_swap(c).wait_send()
        xb_all(c).wait_send()


def on_device(queries, keys, values, grad_out):
    tokens, width = queries.shape
    heads = width // HD
    rows = heads // CH * HD // NH
    devices = lax.axis_size("seq") * lax.axis_size("head")
    scale = 1.0 / math.sqrt(HD * tokens * devices)
    shift = 2.0 ** math.floor(math.log2(scale))
    state = (CH, NH, 2, rows, HD)
    piece = (rows, HD)
    vmem = pltpu.VMEM
    dma = pltpu.SemaphoreType.DMA
    anywhere = pl.BlockSpec(memory_space=pl.ANY)
    macs = tokens * heads * (8 * tokens * HD + 6 * HD * HD)
    results = pl.pallas_call(
        functools.partial(kernel, scale / shift),
        out_shape=[pltpu.VMEM((tokens, width), BF16)] * 4,
        in_specs=[anywhere] * 4,
        scratch_shapes=[
            vmem((4, tokens, width), BF16),
            vmem((4, tokens, width), F32),
            vmem(state, BF16), vmem(state, BF16), vmem(state, BF16), vmem(state, BF16),
            vmem((CH, 2) + piece, F32), vmem((CH,) + piece, F32),
            vmem((CH,) + piece, F32), vmem((CH, NZ) + piece, F32),
            vmem((CH,) + piece, F32), vmem((CH,) + piece, F32),
            dma((CH, 4)), pltpu.SemaphoreType.REGULAR,
            dma((CH,)), dma((CH,)),
            dma((CH,)), dma((CH,)),
            dma((CH, NZ)), dma((CH, NZ)),
            dma((CH,)), dma((CH,)),
            dma((CH,)), dma((CH,)),
        ],
        compiler_params=pltpu.CompilerParams(
            collective_id=0, has_side_effects=True, vmem_limit_bytes=54 * 2**20
        ),
        cost_estimate=pl.CostEstimate(
            flops=2 * macs, bytes_accessed=16 * tokens * width, transcendentals=0
        ),
    )(queries, keys, values, grad_out)
    return tuple(r * jnp.asarray(shift, BF16) for r in results)


def solution(mesh):
    spec = P(("seq", "head"), None)
    return jax.shard_map(
        on_device, mesh=mesh, in_specs=(spec,) * 4, out_specs=(spec,) * 4, check_vma=False
    )
```

```python
import functools
import math

import jax
import jax.numpy as jnp
from jax import lax
from jax.experimental import pallas as pl
from jax.experimental.pallas import tpu as pltpu
from jax.sharding import PartitionSpec as P

HD = 128
NX = 4
NY = 4
NH = NX * NY
NZ = 8
NC = 2
CH = 4
F32 = jnp.float32
BF16 = jnp.bfloat16
MESH = pl.DeviceIdType.MESH


ORDER = (10, 6, 9, 14, 11, 5, 15, 7, 13, 2, 8, 1, 3, 4, 12)
PLAN = (
    ("L", 0), ("A", 0), ("C", 0), ("L", 1), ("A", 1), ("C", 1), ("D", 0), ("E", 0),
    ("A", 2), ("C", 2), ("D", 1), ("E", 1), ("L", 2), ("A", 3), ("C", 3), ("D", 2),
    ("E", 2), ("D", 3), ("E", 3), ("L", 3), ("G", 0), ("G", 1), ("G", 2), ("G", 3),
)


def contract(a, b, da, db):
    return lax.dot_general(a, b, (((da,), (db,)), ((), ())), preferred_element_type=F32)


def kernel(
    scale,
    q_hbm, k_hbm, v_hbm, g_hbm,
    a_out, dq_out, dk_out, dv_out,
    x4, loc,
    mine, xr, xb, xp,
    cs, cr, zs, zr, ds, dr,
    in_sem, told,
    x1s, x1r, c1s, c1r, zss, zrs, c2s, c2r, x2s, x2r,
):
    seq = lax.axis_index("seq")
    head = lax.axis_index("head")
    z = seq // NC
    core = lax.rem(seq, NC)
    y = head // NX
    x = lax.rem(head, NX)
    chunks = xr.shape[0]
    rows = xr.shape[3]
    tokens = x4.shape[1]
    wide = x4.shape[2] // chunks
    pair = 2 * HD

    ins = (q_hbm, k_hbm, v_hbm, g_hbm)
    outs = (a_out, dq_out, dk_out, dv_out)

    def load(c, i):
        cols = pl.ds(c * wide, wide)
        return pltpu.make_async_copy(ins[i].at[:, cols], x4.at[i, :, cols], in_sem.at[c, i])

    def at_z(to):
        return (to * NC + core, head)

    other = (z * NC + 1 - core, head)

    def remote(src, dst, send, recv, to):
        return pltpu.make_async_remote_copy(src, dst, send, recv, device_id=to, device_id_type=MESH)

    def ahead(d):
        return lax.rem(y + d // NX, NY) * NX + lax.rem(x + d % NX, NX)

    def slot(i):
        return lax.rem(y + NY - i // NX, NY) * NX + lax.rem(x + NX - i % NX, NX)

    def x_out(c, d):
        to = ahead(d)
        return remote(mine.at[c, to], xr.at[c, d], x1s.at[c], x1r.at[c], (seq, to))

    def xb_out(c, d):
        to = ahead(d)
        return remote(xb.at[c, to], xp.at[c, head], x2s.at[c], x2r.at[c], (seq, to))

    def x_all(c):
        some = pl.ds(1, NH - 1)
        return remote(mine.at[c, some], xr.at[c, some], x1s.at[c], x1r.at[c], (seq, ahead(1)))

    def xb_all(c):
        some = pl.ds(1, NH - 1)
        return remote(xb.at[c, some], xp.at[c, some], x2s.at[c], x2r.at[c], (seq, ahead(1)))

    def c_swap(c):
        return remote(cs.at[c, 1 - core], cr.at[c], c1s.at[c], c1r.at[c], other)

    def z_out(c, to):
        return remote(zs.at[c], zr.at[c, z], zss.at[c, to], zrs.at[c, z], at_z(to))

    def z_in(c, frm):
        return remote(zs.at[c], zr.at[c, frm], zss.at[c, frm], zrs.at[c, frm], at_z(frm))

    def d_swap(c):
        return remote(ds.at[c], dr.at[c], c2s.at[c], c2r.at[c], other)

    def sends_to(to):
        return jnp.logical_or(
            jnp.logical_and(core == 0, to > z), jnp.logical_and(core == 1, to < z)
        )

    def hears_from(frm):
        return jnp.logical_or(
            jnp.logical_and(core == 0, frm < z), jnp.logical_and(core == 1, frm > z)
        )

    barrier = pltpu.get_barrier_semaphore()

    def greet(to):
        pl.semaphore_signal(barrier, inc=1, device_id=to, device_id_type=MESH)

    for d in range(1, NH):
        greet((z * NC, ahead(d)))
    for d in range(1, NZ):
        greet((lax.rem(z + d, NZ) * NC + 1, head))
    greet(other)

    for c in range(chunks):
        for i in range(4):
            load(c, i).start()

    def part(ref, j):
        return ref[:, j * HD : (j + 1) * HD]

    def each_pair(c, act):
        def body(o, carry):
            cols = pl.ds(pl.multiple_of(c * wide + o * pair, pair), pair)
            act(o, cols, [x4[i, :, cols] for i in range(4)])
            return carry

        lax.fori_loop(0, wide // pair, body, 0)

    slots = HD // rows

    def local_states(c):
        def act(o, cols, qkvg):
            q, k, v, g = qkvg
            for j in range(2):
                kv = contract(part(k, j), part(v, j), 0, 0).astype(BF16)
                rq = contract(part(g, j), part(q, j), 0, 0).astype(BF16)
                for r in range(slots):
                    at = (o * 2 + j) * slots + r
                    mine[c, at, 0] = kv[r * rows : (r + 1) * rows]
                    mine[c, at, 1] = rq[r * rows : (r + 1) * rows]

        each_pair(c, act)

    def local_attention(c):
        t = lax.broadcasted_iota(jnp.int32, (tokens, tokens), 0)
        s = lax.broadcasted_iota(jnp.int32, (tokens, tokens), 1)

        def act(o, cols, qkvg):
            zero = jnp.zeros((tokens, tokens), F32)
            for j in range(2):
                qj, kj, vj, gj = (part(r, j) for r in qkvg)
                here = pl.ds(pl.multiple_of(c * wide + o * pair + j * HD, HD), HD)
                qk = jnp.where(t >= s, contract(qj, kj, 1, 1), zero).astype(BF16)
                loc[0, :, here] = contract(qk, vj, 1, 0)
                gv = jnp.where(t >= s, contract(gj, vj, 1, 1), zero).astype(BF16)
                loc[1, :, here] = contract(gv, kj, 1, 0)
                vg = jnp.where(s >= t, contract(vj, gj, 1, 1), zero).astype(BF16)
                loc[2, :, here] = contract(vg, qj, 1, 0)
                kq = jnp.where(s >= t, contract(kj, qj, 1, 1), zero).astype(BF16)
                loc[3, :, here] = contract(kq, gj, 1, 0)

        each_pair(c, act)

    def finish(c):
        def act(o, cols, qkvg):
            q, k, v, g = qkvg
            for j in range(2):
                here = pl.ds(pl.multiple_of(c * wide + o * pair + j * HD, HD), HD)
                at = pl.ds((o * 2 + j) * slots, slots)
                kv = xp[c, at, 0].reshape(HD, HD)
                rq = xp[c, at, 1].reshape(HD, HD)
                terms = (
                    contract(part(q, j), kv, 1, 0),
                    contract(part(g, j), kv, 1, 1),
                    contract(part(v, j), rq, 1, 0),
                    contract(part(k, j), rq, 1, 1),
                )
                for i in range(4):
                    outs[i][:, here] = (scale * (loc[i, :, here] + terms[i])).astype(BF16)

        each_pair(c, act)

    def stage_a(c):
        xr[c, 0] = mine[c, head]
        x_all(c).wait_recv()
        total = xr[c, 0].astype(F32)
        for d in range(1, NH):
            total += xr[c, d].astype(F32)
        cs[c] = total
        c_swap(c).start()

    def stage_c(c):
        c_swap(c).wait_recv()
        zs[c] = cs[c, core] + cr[c]
        for i in range(NZ):
            @pl.when(sends_to(i))
            def _():
                z_out(c, i).start()

    def stage_d(c):
        ds[c] = jnp.zeros_like(ds[c])
        for i in range(NZ):
            @pl.when(hears_from(i))
            def _():
                z_in(c, i).wait_recv()
                ds[c] += zr[c, i]
        zr[c, z] = ds[c]
        ds[c] += cs[c, core]
        d_swap(c).start()

    def stage_e(c):
        d_swap(c).wait_recv()
        for kind in range(2):
            base = jnp.where(core == kind, zr[c, z], dr[c])
            order = range(NH) if kind == 0 else range(NH - 1, -1, -1)
            for i in order:
                xb[c, i, kind] = base.astype(BF16)
                base = base + xr[c, slot(i), kind].astype(F32)
        for d in ORDER:
            xb_out(c, d).start()
        xp[c, head] = xb[c, head]

    def stage_g(c):
        xb_all(c).wait_recv()
        finish(c)

    for c in range(chunks):
        for i in range(4):
            load(c, i).wait()
        local_states(c)
        if c == 0:
            @pl.when(core == 0)
            def _():
                pl.semaphore_wait(barrier, NC * (NH - 1) + 1)
                pl.semaphore_signal(told, inc=1, device_id=other, device_id_type=MESH)

            @pl.when(core == 1)
            def _():
                pl.semaphore_wait(told, 1)

        for d in ORDER:
            x_out(c, d).start()

    stages = {
        "L": local_attention, "A": stage_a, "C": stage_c, "D": stage_d, "E": stage_e, "G": stage_g,
    }
    def meet_z():
        @pl.when(core == 1)
        def _():
            pl.semaphore_wait(barrier, NC * (NZ - 1) + 1)
            pl.semaphore_signal(told, inc=1, device_id=other, device_id_type=MESH)

        @pl.when(core == 0)
        def _():
            pl.semaphore_wait(told, 1)

    for name, c in PLAN:
        if (name, c) == ("A", 0):
            meet_z()
        stages[name](c)

    for c in range(chunks):
        x_all(c).wait_send()
        c_swap(c).wait_send()
        for i in range(NZ):
            @pl.when(sends_to(i))
            def _():
                z_out(c, i).wait_send()
        d_swap(c).wait_send()
        xb_all(c).wait_send()


def write_out(a, dq, dk, dv, a_hbm, dq_hbm, dk_hbm, dv_hbm, sem):
    pairs = ((a, a_hbm), (dq, dq_hbm), (dk, dk_hbm), (dv, dv_hbm))
    moves = [pltpu.make_async_copy(src, dst, sem.at[i]) for i, (src, dst) in enumerate(pairs)]
    for move in moves:
        move.start()
    for move in moves:
        move.wait()


def on_device(queries, keys, values, grad_out):
    tokens, width = queries.shape
    heads = width // HD
    rows = heads // CH * HD // NH
    devices = lax.axis_size("seq") * lax.axis_size("head")
    scale = 1.0 / math.sqrt(HD * tokens * devices)
    state = (CH, NH, 2, rows, HD)
    piece = (rows, HD)
    vmem = pltpu.VMEM
    dma = pltpu.SemaphoreType.DMA
    anywhere = pl.BlockSpec(memory_space=pl.ANY)
    macs = tokens * heads * (8 * tokens * HD + 6 * HD * HD)
    results = pl.pallas_call(
        functools.partial(kernel, scale),
        out_shape=[pltpu.VMEM((tokens, width), BF16)] * 4,
        in_specs=[anywhere] * 4,
        scratch_shapes=[
            vmem((4, tokens, width), BF16),
            vmem((4, tokens, width), F32),
            vmem(state, BF16), vmem(state, BF16), vmem(state, BF16), vmem(state, BF16),
            vmem((CH, 2) + piece, F32), vmem((CH,) + piece, F32),
            vmem((CH,) + piece, F32), vmem((CH, NZ) + piece, F32),
            vmem((CH,) + piece, F32), vmem((CH,) + piece, F32),
            dma((CH, 4)), pltpu.SemaphoreType.REGULAR,
            dma((CH,)), dma((CH,)),
            dma((CH,)), dma((CH,)),
            dma((CH, NZ)), dma((CH, NZ)),
            dma((CH,)), dma((CH,)),
            dma((CH,)), dma((CH,)),
        ],
        compiler_params=pltpu.CompilerParams(
            collective_id=0, has_side_effects=True, vmem_limit_bytes=54 * 2**20
        ),
        cost_estimate=pl.CostEstimate(
            flops=2 * macs, bytes_accessed=16 * tokens * width, transcendentals=0
        ),
    )(queries, keys, values, grad_out)
    written = pl.pallas_call(
        write_out,
        out_shape=[jax.ShapeDtypeStruct((tokens, width), BF16)] * 4,
        in_specs=[anywhere] * 4,
        out_specs=[anywhere] * 4,
        scratch_shapes=[dma((4,))],
        compiler_params=pltpu.CompilerParams(vmem_limit_bytes=4 * 2**20),
    )(*results)
    return tuple(written)


def solution(mesh):
    spec = P(("seq", "head"), None)
    return jax.shard_map(
        on_device, mesh=mesh, in_specs=(spec,) * 4, out_specs=(spec,) * 4, check_vma=False
    )
```

```python
import functools
import math

import jax
import jax.numpy as jnp
from jax import lax
from jax.experimental import pallas as pl
from jax.experimental.pallas import tpu as pltpu
from jax.sharding import PartitionSpec as P

HD = 128
NX = 4
NY = 4
NH = NX * NY
NZ = 8
NC = 2
CH = 8
CHUNKS = ((0, 1), (1, 1), (2, 2), (4, 2), (6, 1), (7, 1))
F32 = jnp.float32
BF16 = jnp.bfloat16
MESH = pl.DeviceIdType.MESH


ORDER = (10, 6, 9, 14, 11, 5, 15, 7, 13, 2, 8, 1, 3, 4, 12)
PLAN = (
    ("L", 0), ("A", 0), ("C", 0), ("L", 1), ("A", 1), ("C", 1), ("D", 0), ("E", 0),
    ("L", 2), ("A", 2), ("C", 2), ("D", 1), ("E", 1), ("L", 3), ("A", 3), ("C", 3),
    ("D", 2), ("E", 2), ("A", 4), ("C", 4), ("D", 3), ("E", 3), ("A", 5), ("C", 5),
    ("D", 4), ("E", 4), ("D", 5), ("E", 5), ("L", 4), ("L", 5), ("G", 0), ("G", 1),
    ("G", 2), ("G", 3), ("G", 4), ("G", 5),
)


def contract(a, b, da, db):
    return lax.dot_general(a, b, (((da,), (db,)), ((), ())), preferred_element_type=F32)


def kernel(
    scale,
    q_hbm, k_hbm, v_hbm, g_hbm,
    a_out, dq_out, dk_out, dv_out,
    x4, loc,
    mine, xr, xb, xp,
    cs, cr, zs, zr, ds, dr,
    in_sem, told,
    x1s, x1r, c1s, c1r, zss, zrs, c2s, c2r, x2s, x2r,
):
    seq = lax.axis_index("seq")
    head = lax.axis_index("head")
    z = seq // NC
    core = lax.rem(seq, NC)
    y = head // NX
    x = lax.rem(head, NX)
    groups = xr.shape[0]
    rows = xr.shape[3]
    chunks = range(len(CHUNKS))
    runs = [pl.ds(first, many) for first, many in CHUNKS]
    tokens = x4.shape[1]
    wide = x4.shape[2] // groups
    pair = 2 * HD

    ins = (q_hbm, k_hbm, v_hbm, g_hbm)
    outs = (a_out, dq_out, dk_out, dv_out)

    def load(c, i):
        first, many = CHUNKS[c]
        cols = pl.ds(first * wide, many * wide)
        return pltpu.make_async_copy(ins[i].at[:, cols], x4.at[i, :, cols], in_sem.at[c, i])

    def at_z(to):
        return (to * NC + core, head)

    other = (z * NC + 1 - core, head)

    def remote(src, dst, send, recv, to):
        return pltpu.make_async_remote_copy(src, dst, send, recv, device_id=to, device_id_type=MESH)

    def ahead(d):
        return lax.rem(y + d // NX, NY) * NX + lax.rem(x + d % NX, NX)

    def slot(i):
        return lax.rem(y + NY - i // NX, NY) * NX + lax.rem(x + NX - i % NX, NX)

    def x_out(c, d):
        to = ahead(d)
        return remote(mine.at[runs[c], to], xr.at[runs[c], d], x1s.at[c], x1r.at[c], (seq, to))

    def xb_out(c, d):
        to = ahead(d)
        return remote(xb.at[runs[c], to], xp.at[runs[c], head], x2s.at[c], x2r.at[c], (seq, to))

    def x_all(c):
        some = pl.ds(1, NH - 1)
        return remote(mine.at[runs[c], some], xr.at[runs[c], some], x1s.at[c], x1r.at[c], (seq, ahead(1)))

    def xb_all(c):
        some = pl.ds(1, NH - 1)
        return remote(xb.at[runs[c], some], xp.at[runs[c], some], x2s.at[c], x2r.at[c], (seq, ahead(1)))

    def c_swap(c):
        return remote(cs.at[runs[c], 1 - core], cr.at[runs[c]], c1s.at[c], c1r.at[c], other)

    def z_out(c, to):
        return remote(zs.at[runs[c]], zr.at[runs[c], z], zss.at[c, to], zrs.at[c, z], at_z(to))

    def z_in(c, frm):
        return remote(zs.at[runs[c]], zr.at[runs[c], frm], zss.at[c, frm], zrs.at[c, frm], at_z(frm))

    def d_swap(c):
        return remote(ds.at[runs[c]], dr.at[runs[c]], c2s.at[c], c2r.at[c], other)

    def sends_to(to):
        return jnp.logical_or(
            jnp.logical_and(core == 0, to > z), jnp.logical_and(core == 1, to < z)
        )

    def hears_from(frm):
        return jnp.logical_or(
            jnp.logical_and(core == 0, frm < z), jnp.logical_and(core == 1, frm > z)
        )

    barrier = pltpu.get_barrier_semaphore()

    def greet(to):
        pl.semaphore_signal(barrier, inc=1, device_id=to, device_id_type=MESH)

    for d in range(1, NH):
        greet((z * NC, ahead(d)))
    for d in range(1, NZ):
        greet((lax.rem(z + d, NZ) * NC + 1, head))
    greet(other)

    for c in chunks:
        for i in range(4):
            load(c, i).start()

    def part(ref, j):
        return ref[:, j * HD : (j + 1) * HD]

    def each_pair(c, act):
        first, many = CHUNKS[c]
        each = wide // pair

        def body(i, carry):
            cols = pl.ds(pl.multiple_of((first * each + i) * pair, pair), pair)
            act(first + i // each, lax.rem(i, each), [x4[j, :, cols] for j in range(4)])
            return carry

        lax.fori_loop(0, many * each, body, 0)

    slots = HD // rows

    def local_states(c):
        def act(u, o, qkvg):
            q, k, v, g = qkvg
            for j in range(2):
                kv = contract(part(k, j), part(v, j), 0, 0).astype(BF16)
                rq = contract(part(g, j), part(q, j), 0, 0).astype(BF16)
                for r in range(slots):
                    at = (o * 2 + j) * slots + r
                    mine[u, at, 0] = kv[r * rows : (r + 1) * rows]
                    mine[u, at, 1] = rq[r * rows : (r + 1) * rows]

        each_pair(c, act)

    def local_attention(c):
        t = lax.broadcasted_iota(jnp.int32, (tokens, tokens), 0)
        s = lax.broadcasted_iota(jnp.int32, (tokens, tokens), 1)

        def act(u, o, qkvg):
            zero = jnp.zeros((tokens, tokens), F32)
            for j in range(2):
                qj, kj, vj, gj = (part(r, j) for r in qkvg)
                here = pl.ds(pl.multiple_of(u * wide + o * pair + j * HD, HD), HD)
                qk = jnp.where(t >= s, contract(qj, kj, 1, 1), zero).astype(BF16)
                loc[0, :, here] = contract(qk, vj, 1, 0)
                gv = jnp.where(t >= s, contract(gj, vj, 1, 1), zero).astype(BF16)
                loc[1, :, here] = contract(gv, kj, 1, 0)
                vg = jnp.where(s >= t, contract(vj, gj, 1, 1), zero).astype(BF16)
                loc[2, :, here] = contract(vg, qj, 1, 0)
                kq = jnp.where(s >= t, contract(kj, qj, 1, 1), zero).astype(BF16)
                loc[3, :, here] = contract(kq, gj, 1, 0)

        each_pair(c, act)

    def finish(c):
        def act(u, o, qkvg):
            q, k, v, g = qkvg
            for j in range(2):
                here = pl.ds(pl.multiple_of(u * wide + o * pair + j * HD, HD), HD)
                at = pl.ds((o * 2 + j) * slots, slots)
                kv = xp[u, at, 0].reshape(HD, HD)
                rq = xp[u, at, 1].reshape(HD, HD)
                terms = (
                    contract(part(q, j), kv, 1, 0),
                    contract(part(g, j), kv, 1, 1),
                    contract(part(v, j), rq, 1, 0),
                    contract(part(k, j), rq, 1, 1),
                )
                for i in range(4):
                    outs[i][:, here] = (scale * (loc[i, :, here] + terms[i])).astype(BF16)

        each_pair(c, act)

    def stage_a(c):
        run = runs[c]
        xr[run, 0] = mine[run, head]
        x_all(c).wait_recv()
        total = xr[run, 0].astype(F32)
        for d in range(1, NH):
            total += xr[run, d].astype(F32)
        cs[run] = total
        c_swap(c).start()

    def stage_c(c):
        run = runs[c]
        c_swap(c).wait_recv()
        zs[run] = cs[run, core] + cr[run]
        for i in range(NZ):
            @pl.when(sends_to(i))
            def _():
                z_out(c, i).start()

    def stage_d(c):
        run = runs[c]
        ds[run] = jnp.zeros_like(ds[run])
        for i in range(NZ):
            @pl.when(hears_from(i))
            def _():
                z_in(c, i).wait_recv()
                ds[run] += zr[run, i]
        zr[run, z] = ds[run]
        ds[run] += cs[run, core]
        d_swap(c).start()

    def stage_e(c):
        run = runs[c]
        d_swap(c).wait_recv()
        for kind in range(2):
            base = jnp.where(core == kind, zr[run, z], dr[run])
            order = range(NH) if kind == 0 else range(NH - 1, -1, -1)
            for i in order:
                xb[run, i, kind] = base.astype(BF16)
                base = base + xr[run, slot(i), kind].astype(F32)
        for d in ORDER:
            xb_out(c, d).start()
        xp[run, head] = xb[run, head]

    def stage_g(c):
        xb_all(c).wait_recv()
        finish(c)

    for c in chunks:
        for i in range(4):
            load(c, i).wait()
        local_states(c)
        if c == 0:
            @pl.when(core == 0)
            def _():
                pl.semaphore_wait(barrier, NC * (NH - 1) + 1)
                pl.semaphore_signal(told, inc=1, device_id=other, device_id_type=MESH)

            @pl.when(core == 1)
            def _():
                pl.semaphore_wait(told, 1)

        for d in ORDER:
            x_out(c, d).start()

    stages = {
        "L": local_attention, "A": stage_a, "C": stage_c, "D": stage_d, "E": stage_e, "G": stage_g,
    }
    def meet_z():
        @pl.when(core == 1)
        def _():
            pl.semaphore_wait(barrier, NC * (NZ - 1) + 1)
            pl.semaphore_signal(told, inc=1, device_id=other, device_id_type=MESH)

        @pl.when(core == 0)
        def _():
            pl.semaphore_wait(told, 1)

    for name, c in PLAN:
        if (name, c) == ("A", 0):
            meet_z()
        stages[name](c)

    for c in chunks:
        x_all(c).wait_send()
        c_swap(c).wait_send()
        for i in range(NZ):
            @pl.when(sends_to(i))
            def _():
                z_out(c, i).wait_send()
        d_swap(c).wait_send()
        xb_all(c).wait_send()


def write_out(a, dq, dk, dv, a_hbm, dq_hbm, dk_hbm, dv_hbm, sem):
    pairs = ((a, a_hbm), (dq, dq_hbm), (dk, dk_hbm), (dv, dv_hbm))
    moves = [pltpu.make_async_copy(src, dst, sem.at[i]) for i, (src, dst) in enumerate(pairs)]
    for move in moves:
        move.start()
    for move in moves:
        move.wait()


def on_device(queries, keys, values, grad_out):
    tokens, width = queries.shape
    heads = width // HD
    rows = heads // CH * HD // NH
    devices = lax.axis_size("seq") * lax.axis_size("head")
    scale = 1.0 / math.sqrt(HD * tokens * devices)
    state = (CH, NH, 2, rows, HD)
    piece = (rows, HD)
    vmem = pltpu.VMEM
    dma = pltpu.SemaphoreType.DMA
    anywhere = pl.BlockSpec(memory_space=pl.ANY)
    macs = tokens * heads * (8 * tokens * HD + 6 * HD * HD)
    results = pl.pallas_call(
        functools.partial(kernel, scale),
        out_shape=[pltpu.VMEM((tokens, width), BF16)] * 4,
        in_specs=[anywhere] * 4,
        scratch_shapes=[
            vmem((4, tokens, width), BF16),
            vmem((4, tokens, width), F32),
            vmem(state, BF16), vmem(state, BF16), vmem(state, BF16), vmem(state, BF16),
            vmem((CH, 2) + piece, F32), vmem((CH,) + piece, F32),
            vmem((CH,) + piece, F32), vmem((CH, NZ) + piece, F32),
            vmem((CH,) + piece, F32), vmem((CH,) + piece, F32),
            dma((len(CHUNKS), 4)), pltpu.SemaphoreType.REGULAR,
            dma((len(CHUNKS),)), dma((len(CHUNKS),)),
            dma((len(CHUNKS),)), dma((len(CHUNKS),)),
            dma((len(CHUNKS), NZ)), dma((len(CHUNKS), NZ)),
            dma((len(CHUNKS),)), dma((len(CHUNKS),)),
            dma((len(CHUNKS),)), dma((len(CHUNKS),)),
        ],
        compiler_params=pltpu.CompilerParams(
            collective_id=0, has_side_effects=True, vmem_limit_bytes=54 * 2**20
        ),
        cost_estimate=pl.CostEstimate(
            flops=2 * macs, bytes_accessed=16 * tokens * width, transcendentals=0
        ),
    )(queries, keys, values, grad_out)
    written = pl.pallas_call(
        write_out,
        out_shape=[jax.ShapeDtypeStruct((tokens, width), BF16)] * 4,
        in_specs=[anywhere] * 4,
        out_specs=[anywhere] * 4,
        scratch_shapes=[dma((4,))],
        compiler_params=pltpu.CompilerParams(vmem_limit_bytes=4 * 2**20),
    )(*results)
    return tuple(written)


def solution(mesh):
    spec = P(("seq", "head"), None)
    return jax.shard_map(
        on_device, mesh=mesh, in_specs=(spec,) * 4, out_specs=(spec,) * 4, check_vma=False
    )
```
